32 devices in a mesh: head: 8 (over z, y), query: 4 (over x, core).
Axes of the slice: x: 2, y: 2, z: 4, core: 2. Of those that a mesh axis runs over, the one named last changes fastest.
Arguments:
- queries: bfloat16 [4096, 32, 128], P(('query', 'head')), may hold values from -100 to 100
- keys: bfloat16 [4096, 4, 128], P(('query', 'head')), may hold values from -4 to 4
- values: bfloat16 [4096, 4, 128], P(('query', 'head')), may hold values from -6 to 6
- attention_out: bfloat16 [4096, 32, 128], P(('query', 'head')), may hold values from -3 to 3
- out_grad: bfloat16 [4096, 32, 128], P(('query', 'head')), may hold values from -6 to 6
- span_order: int32 [4, 2], replicated, may hold values from 0 to 7, as said below
- doc_lengths: int32 [16], replicated, may hold values from 1 to 512, 4096 in all
Outputs:
- query_grad: bfloat16 [4096, 32, 128], P(('query', 'head'))
- key_grad: bfloat16 [4096, 4, 128], P(('query', 'head'))
- value_grad: bfloat16 [4096, 4, 128], P(('query', 'head'))
The draws below stay inside these ranges and needn't reach their ends.
Inputs may be any that keep to these rules, and one draw needn't show every extreme that they name: `span_order`: every number from 0 to 7 appears exactly once; the two numbers of a row sum to 7, in either order. `doc_lengths`: the lengths sum to 4096.
All inputs are finite; a program needn't handle non-finite values.
Results may differ from the reference program's by a relative error of at most 0.0058.
Values may be sent and summed in bfloat16 or wider, within the bound.
A program may use at most 128 MiB of HBM per device.

```python
import math
import jax
import jax.numpy as jnp
import numpy as np
from jax import lax

QUERY_HEADS = 32
KEY_VALUE_HEADS = 4
HEAD_WIDTH = 128
GROUP = 8
QROWS = 1024
TOKEN_COUNT = 4096
SPAN = 512
DOC_MOST = 512
DOCS = 16
N_HEAD = 8


def drawn_pair(key):
    base = jax.random.fold_in(key, 7)
    random_key_seed, query_seed = jax.random.split(base, 2)
    sampled_keys = jnp.clip(jax.random.normal(random_key_seed, (TOKEN_COUNT, KEY_VALUE_HEADS, HEAD_WIDTH), jnp.float32), -4.0, 4.0)
    queries_draw = jnp.clip(jax.random.normal(query_seed, (TOKEN_COUNT, QUERY_HEADS, HEAD_WIDTH), jnp.float32), -4.0, 4.0)
    return (queries_draw, sampled_keys)


def draw_queries(key, part):
    return drawn_pair(key)[0].astype(jnp.bfloat16)


def draw_keys(key, part):
    return drawn_pair(key)[1].astype(jnp.bfloat16)


def draw_span_order(key, part):
    pair_count = TOKEN_COUNT // QROWS
    order_seed, swap_seed = jax.random.split(jax.random.fold_in(key, 11))
    early_span = jax.random.permutation(order_seed, jnp.arange(pair_count, dtype=jnp.int32))
    late_span = 2 * pair_count - 1 - early_span
    swapped = jax.random.randint(swap_seed, (pair_count,), 0, 2)
    leading = jnp.where(swapped == 1, late_span, early_span)
    trailing = jnp.where(swapped == 1, early_span, late_span)
    return jnp.stack([leading, trailing], axis=1).astype(jnp.int32)


def block_scale(stream_key, extent, cuts, smallest, largest):
    level, own = 1.0, jax.random.fold_in(stream_key, 6)
    for axis_at, shards_of in cuts:
        draws = jnp.exp(jax.random.uniform(jax.random.fold_in(own, axis_at), (shards_of,), jnp.float32, smallest / len(cuts), largest / len(cuts)))
        level = level * jnp.repeat(draws, extent[axis_at] // shards_of).reshape([-1 if axis == axis_at else 1 for axis in range(len(extent))])
    return level


def length_profile(number_of, total, most, lean):
    portions = [(1 << 20) // math.isqrt(rank ** lean) + 1 for rank in range(2, number_of + 1)]
    spare, counts = total - most - (number_of - 1), [1] * (number_of - 1)
    while spare > 0:
        free = [i for i in range(number_of - 1) if counts[i] < most]
        mass, remaining = sum([portions[i] for i in free]), spare
        for i in free:
            addition = min(most - counts[i], max(1, remaining * portions[i] // mass), spare)
            counts[i] = counts[i] + addition
            spare = spare - addition
    return np.array([most] + counts)


def ragged(rng, number_of, total, bound, slope):
    if number_of == 2:
        one = jax.random.randint(rng, (), max(1, total - bound), min(bound, total - 1) + 1)
        return jnp.stack([one, total - one])
    tallies = jnp.asarray(length_profile(number_of, total, bound, slope), jnp.int32)
    pairs = (number_of - 1) // 2
    source_of, receiver = tallies[1:1 + 2 * pairs:2], tallies[2:2 + 2 * pairs:2]
    margin = jnp.minimum(source_of - 1, bound - receiver)
    passed = jax.random.randint(jax.random.fold_in(rng, 1), (pairs,), 0, 1 << 20) % (margin + 1)
    tallies = tallies.at[1:1 + 2 * pairs:2].set(source_of - passed).at[2:2 + 2 * pairs:2].set(receiver + passed)
    return tallies[jax.random.permutation(jax.random.fold_in(rng, 2), number_of)]


def scatter_about(stream_key, extent, scale, reach, cuts=(), kind=jnp.bfloat16):
    drawn = jax.random.normal(stream_key, extent, jnp.float32) * scale
    if len(cuts) > 0:
        drawn = block_scale(stream_key, extent, cuts, -0.22, 0.18) * drawn
    return jnp.clip(drawn, min=-reach, max=reach).astype(kind)


def setup_inputs(seed: int = 0) -> dict:
    arg_keys = jax.random.split(jax.random.key(seed), 8)
    queries = draw_queries(jax.random.fold_in(arg_keys[7], 71), 0)
    keys = draw_keys(jax.random.fold_in(arg_keys[7], 71), 0)
    values = scatter_about(arg_keys[2], (TOKEN_COUNT, KEY_VALUE_HEADS, HEAD_WIDTH), 1.0, 6.0, ((0, 32),))
    attention_out = scatter_about(arg_keys[3], (TOKEN_COUNT, QUERY_HEADS, HEAD_WIDTH), 0.5, 3.0, ((0, 32),))
    out_grad = scatter_about(arg_keys[4], (TOKEN_COUNT, QUERY_HEADS, HEAD_WIDTH), 1.0, 6.0, ((0, 32),))
    span_order = draw_span_order(jax.random.fold_in(arg_keys[7], 71), 0)
    doc_lengths = ragged(arg_keys[6], DOCS, TOKEN_COUNT, DOC_MOST, 2).astype(jnp.int32)
    return {"queries": queries, "keys": keys, "values": values, "attention_out": attention_out, "out_grad": out_grad, "span_order": span_order, "doc_lengths": doc_lengths}


masked = -1e30


def positions(span_order, doc_lengths, rows_each):
    span_rows = rows_each // 2
    within = jnp.arange(span_rows, dtype=jnp.int32)
    pos_all = (span_order[:, :, None] * span_rows + within[None, None, :]).reshape(-1).astype(jnp.int32)
    doc_ends = jnp.cumsum(doc_lengths)[:-1]
    doc_all = jnp.sum((pos_all[:, None] >= doc_ends[None, :]).astype(jnp.int32), axis=1).astype(jnp.int32)
    return pos_all, doc_all


def reference(queries, keys, values, attention_out, out_grad, span_order, doc_lengths):
    pos_all, doc_all = positions(span_order, doc_lengths, QROWS)
    row_of = jnp.zeros((TOKEN_COUNT,), jnp.int32).at[pos_all].set(jnp.arange(TOKEN_COUNT, dtype=jnp.int32))
    doc_sorted = doc_all[row_of]
    window = min(TOKEN_COUNT, SPAN + DOC_MOST)
    span_count = TOKEN_COUNT // SPAN
    factor = HEAD_WIDTH ** -0.5
    head_copies = max(N_HEAD // KEY_VALUE_HEADS, 1)

    def per_head(head):
        kv_index = head // GROUP
        query_pos = queries[:, head, :][row_of]
        key_pos = keys[:, kv_index, :][row_of]
        value_pos = values[:, kv_index, :][row_of]
        grad_pos = out_grad[:, head, :][row_of]
        out_pos = attention_out[:, head, :][row_of]
        delta_pos = jnp.sum(out_pos.astype(jnp.float32) * grad_pos.astype(jnp.float32), axis=-1)

        def step(carry, span):
            key_acc, value_acc = carry
            first = (span * SPAN).astype(jnp.int32)
            start = jnp.clip(first + SPAN - window, 0, TOKEN_COUNT - window).astype(jnp.int32)
            query_mat = lax.dynamic_slice_in_dim(query_pos, first, SPAN)
            grad_mat = lax.dynamic_slice_in_dim(grad_pos, first, SPAN)
            delta = lax.dynamic_slice_in_dim(delta_pos, first, SPAN)
            query_doc = lax.dynamic_slice_in_dim(doc_sorted, first, SPAN)
            key_mat = lax.dynamic_slice_in_dim(key_pos, start, window)
            value_mat = lax.dynamic_slice_in_dim(value_pos, start, window)
            key_doc = lax.dynamic_slice_in_dim(doc_sorted, start, window)
            query_place = first + jnp.arange(SPAN, dtype=jnp.int32)
            key_place = start + jnp.arange(window, dtype=jnp.int32)
            allowed = (key_place[None, :] <= query_place[:, None]) & (key_doc[None, :] == query_doc[:, None])
            scores = jnp.where(allowed, jnp.dot(query_mat, key_mat.T, preferred_element_type=jnp.float32) * factor, masked)
            row_max = jnp.max(scores, axis=-1)
            row_sum = jnp.sum(jnp.where(allowed, jnp.exp(scores - row_max[:, None]), 0.0), axis=-1)
            log_sum = row_max + jnp.log(row_sum)
            probability = jnp.where(allowed, jnp.exp(scores - log_sum[:, None]), 0.0)
            grad_prob = jnp.dot(grad_mat, value_mat.T, preferred_element_type=jnp.float32)
            grad_score = (probability * (grad_prob - delta[:, None])).astype(jnp.bfloat16)
            query_part = jnp.dot(grad_score, key_mat, preferred_element_type=jnp.float32) * factor
            key_part = jnp.dot(grad_score.T, query_mat, preferred_element_type=jnp.float32) * factor
            value_part = jnp.dot(probability.astype(jnp.bfloat16).T, grad_mat, preferred_element_type=jnp.float32)
            key_acc = lax.dynamic_update_slice_in_dim(key_acc, lax.dynamic_slice_in_dim(key_acc, start, window) + key_part, start, 0)
            value_acc = lax.dynamic_update_slice_in_dim(value_acc, lax.dynamic_slice_in_dim(value_acc, start, window) + value_part, start, 0)
            return (key_acc, value_acc), query_part

        zero = jnp.zeros((TOKEN_COUNT, HEAD_WIDTH), jnp.float32)
        (key_acc, value_acc), query_parts = lax.scan(step, (zero, zero), jnp.arange(span_count, dtype=jnp.int32))
        query_sorted = query_parts.reshape(TOKEN_COUNT, HEAD_WIDTH)
        return query_sorted[pos_all], key_acc[pos_all], value_acc[pos_all]

    query_all, key_all, value_all = lax.map(per_head, jnp.arange(QUERY_HEADS, dtype=jnp.int32))

    def collect(gradient_list):
        value_partial = gradient_list.reshape(KEY_VALUE_HEADS, head_copies, QUERY_HEADS // (KEY_VALUE_HEADS * head_copies), TOKEN_COUNT, HEAD_WIDTH).sum(axis=2)
        value_partial = lax.optimization_barrier(value_partial.astype(jnp.bfloat16)).astype(jnp.float32)
        return jnp.transpose(value_partial.sum(axis=1), (1, 0, 2)).astype(jnp.bfloat16)

    query_grad = jnp.transpose(query_all, (1, 0, 2)).astype(jnp.bfloat16)
    return query_grad, collect(key_all), collect(value_all)
```

```python
import functools
import math

import jax
import jax.numpy as jnp
from jax import lax
from jax.experimental import pallas as pl
from jax.experimental.pallas import tpu as pltpu
from jax.sharding import PartitionSpec as P

masked = -1e30


def kernel(sizes, order, lengths, kv, query, out_fwd, grad, dquery, dkv, window, cand, picked, prev_out,
           bias, delta, q_rows, g_rows, p_tile, s_tile, partial, sent, came, prev_sum, half_out, half_in,
           back_out, back_in, last_out, last_in, swap_s, swap_r, pick_s, pick_r, prev_s, prev_r, ring_s, ring_r,
           dring_s, dring_r, dprev_s, dprev_r, dpick_s, dpick_r, dswap_s, dswap_r):
    copies, blocks = sizes
    kv_heads, _, rows, width = kv.shape
    group = query.shape[2]
    lanes = rows * group
    keys_seen = (blocks + 1) * rows
    chunk = min(256, lanes)
    token_chunk = chunk // group
    factor = width ** -0.5
    f32, bf16 = jnp.float32, jnp.bfloat16

    mine = lax.axis_index("query")
    head = lax.axis_index("head")
    half, place = lax.div(head, blocks), lax.rem(head, blocks)
    other = 1 - half
    sibling = {"head": other * blocks + place}

    def ahead(d):
        return lax.rem(mine + d, copies)

    def behind(d):
        return lax.rem(mine + (copies - d), copies)

    def lower(t):
        return {"head": half * blocks + lax.rem(place + (blocks - t), blocks)}

    def upper(t):
        return {"head": half * blocks + lax.rem(place + t, blocks)}

    def copy(src, dst, send, recv, to):
        return pltpu.make_async_remote_copy(
            src_ref=src, dst_ref=dst, send_sem=send, recv_sem=recv, device_id=to,
            device_id_type=pl.DeviceIdType.MESH)

    barrier = pltpu.get_barrier_semaphore()
    partners = [sibling]
    partners += [{"query": ahead(d)} for d in range(1, copies)]
    partners += [upper(t) for t in range(1, blocks)]
    for to in partners:
        pl.semaphore_signal(barrier, inc=1, device_id=to, device_id_type=pl.DeviceIdType.MESH)
    pl.semaphore_wait(barrier, len(partners))

    def swap(g):
        return copy(kv.at[g, other], cand.at[g, half], swap_s.at[g], swap_r.at[g], sibling)

    def pick(g, d):
        return copy(picked.at[g, d - 1], cand.at[g, d + 1], pick_s.at[g, d - 1], pick_r.at[g, d - 1],
                    {"query": ahead(d)})

    def prev(g):
        return copy(prev_out.at[g], window.at[g, 0, half], prev_s.at[g], prev_r.at[g], sibling)

    def ring(g, t, own):
        src = kv.at[g] if own else window.at[g, 0]
        return copy(src, window.at[g, t], ring_s.at[g, t - 1], ring_r.at[g, t - 1], lower(t))

    def dring(g, t):
        return copy(sent.at[g, t - 1], came.at[g, t - 1], dring_s.at[g, t - 1], dring_r.at[g, t - 1], upper(t))

    def dprev(g):
        return copy(half_out.at[g], half_in.at[g], dprev_s.at[g], dprev_r.at[g], sibling)

    def dpick(g, d):
        return copy(back_out.at[g, d - 1], back_in.at[g, d - 1], dpick_s.at[g, d - 1], dpick_r.at[g, d - 1],
                    {"query": behind(d)})

    def dswap(g):
        return copy(last_out.at[g], last_in.at[g], dswap_s.at[g], dswap_r.at[g], sibling)

    def each(body):
        def step(g, _):
            body(g)
            return 0
        lax.fori_loop(0, kv_heads, step, 0)

    def source(which):
        wanted = order[mine, which] - 1
        slot = jnp.int32(-1)
        for i in range(2):
            slot = jnp.where(order[mine, i] == wanted, i, slot)
        for d in range(1, copies):
            there = behind(d)
            hit = (order[there, 0] == wanted) | (order[there, 1] == wanted)
            slot = jnp.where(hit, d + 1, slot)
        return slot

    def taken(d):
        there, after = ahead(d), order[mine, 1] + 1
        return (order[there, 0] == after) | (order[there, 1] == after)

    slots = [source(0), source(1)]
    takes = [taken(d) for d in range(1, copies)]

    def first(g):
        swap(g).start()
        for t in range(1, blocks):
            @pl.when(place < t)
            def _():
                ring(g, t, True).start()
    each(first)

    begin = order[mine, half] * (blocks * rows) + place * rows
    row = lax.div(lax.broadcasted_iota(jnp.int32, (1, lanes), 1), jnp.int32(group))
    pos = begin + row

    def bound(i, carry):
        end, low = carry
        end = end + lengths[i]
        return end, jnp.where(pos >= end, end, low)

    _, low = lax.fori_loop(0, lengths.shape[0] - 1, bound, (jnp.int32(0), jnp.zeros_like(pos)))
    low = low - begin + blocks * rows

    def own_and_delta(g):
        cand[g, half] = kv[g, half]
        window[g, blocks] = kv[g]
        product = out_fwd[:, g].astype(f32) * grad[:, g].astype(f32)
        delta[g] = jnp.sum(product.reshape(lanes, width).T, axis=0, keepdims=True)
    each(own_and_delta)

    def choose(g):
        swap(g).wait_recv()
        for d in range(1, copies):
            picked[g, d - 1] = jnp.where(takes[d - 1], cand[g, 1].astype(f32), cand[g, 0].astype(f32)).astype(bf16)
            pick(g, d).start()
    each(choose)

    for c in range(0, lanes, chunk):
        at = lax.broadcasted_iota(jnp.int32, (keys_seen, chunk), 0)
        seen = (at >= low[:, c:c + chunk]) & (at <= row[:, c:c + chunk] + blocks * rows)
        bias[:, c:c + chunk] = jnp.where(seen, 0.0, masked)

    def settle(g):
        for d in range(1, copies):
            pick(g, d).wait_recv()
        both = []
        for i in range(2):
            value = cand[g, 0].astype(f32)
            for k in range(1, copies + 1):
                value = jnp.where(slots[i] == k, cand[g, k].astype(f32), value)
            both.append(value)
        window[g, 0, half] = jnp.where(half == 0, both[0], both[1]).astype(bf16)
        prev_out[g] = jnp.where(half == 0, both[1], both[0]).astype(bf16)
        prev(g).start()
    each(settle)

    def spread(g):
        prev(g).wait_recv()
        for t in range(1, blocks):
            @pl.when(place >= t)
            def _():
                ring(g, t, False).start()
    each(spread)

    def gradients(g):
        for t in range(1, blocks):
            ring(g, t, True).wait_recv()
        q_rows[...] = query[:, g].astype(f32).reshape(lanes, width).astype(bf16)
        g_rows[...] = grad[:, g].astype(f32).reshape(lanes, width).astype(bf16)
        key = window[g, :, 0].reshape(keys_seen, width)
        value = window[g, :, 1].reshape(keys_seen, width)
        key_t = key.astype(f32).T.astype(bf16)
        across = (((1,), (1,)), ((), ()))
        for c in range(0, lanes, chunk):
            cols = slice(c, c + chunk)
            score = lax.dot_general(key, q_rows[cols, :], across, preferred_element_type=f32)
            score = score * (factor * math.log2(math.e)) + bias[:, cols]
            power = jnp.exp2(score - jnp.max(score, axis=0, keepdims=True))
            prob = power * (1.0 / jnp.sum(power, axis=0, keepdims=True))
            grad_prob = lax.dot_general(value, g_rows[cols, :], across, preferred_element_type=f32)
            grad_score = (prob * (grad_prob - delta[g, :, cols])).astype(bf16)
            p_tile[:, cols] = prob.astype(bf16)
            s_tile[:, cols] = grad_score
            dq = jnp.dot(key_t, grad_score, preferred_element_type=f32).T * factor
            first_token = c // group
            dquery[first_token:first_token + token_chunk, g] = dq.reshape(token_chunk, group, width).astype(bf16)
        dk = jnp.dot(s_tile[...], q_rows[...], preferred_element_type=f32) * factor
        dv = jnp.dot(p_tile[...], g_rows[...], preferred_element_type=f32)
        for kind, total in enumerate((dk, dv)):
            total = total.reshape(blocks + 1, rows, width)
            partial[g, 0, kind] = total[0]
            partial[g, 1, kind] = total[blocks]
            sent[g, :, kind] = total[1:blocks].astype(bf16)
        for t in range(1, blocks):
            dring(g, t).start()

    def collect(g):
        earlier, own = partial[g, 0], partial[g, 1]
        for t in range(1, blocks):
            dring(g, t).wait_recv()
            term = came[g, t - 1].astype(f32)
            earlier = earlier + jnp.where(place >= t, term, 0.0)
            own = own + jnp.where(place < t, term, 0.0)
        partial[g, 1] = own
        low_kind = jnp.where(half == 0, earlier[0], earlier[1])
        prev_sum[g] = low_kind.astype(bf16)
        half_out[g] = jnp.where(half == 0, earlier[1], earlier[0]).astype(bf16)
        dprev(g).start()

    def send_back(g):
        dprev(g).wait_recv()
        here, there = prev_sum[g].astype(f32), half_in[g].astype(f32)
        both = [jnp.where(half == 0, here, there), jnp.where(half == 0, there, here)]
        for d in range(1, copies):
            term = jnp.where(slots[0] == d + 1, both[0], 0.0) + jnp.where(slots[1] == d + 1, both[1], 0.0)
            back_out[g, d - 1] = term.astype(bf16)
            dpick(g, d).start()

    def add_up(g):
        here, there = prev_sum[g].astype(f32), half_in[g].astype(f32)
        both = [jnp.where(half == 0, here, there), jnp.where(half == 0, there, here)]
        totals = []
        for i in range(2):
            totals.append(jnp.where(slots[0] == i, both[0], 0.0) + jnp.where(slots[1] == i, both[1], 0.0))
        for d in range(1, copies):
            dpick(g, d).wait_recv()
            term = back_in[g, d - 1].astype(f32)
            totals[1] = totals[1] + jnp.where(takes[d - 1], term, 0.0)
            totals[0] = totals[0] + jnp.where(takes[d - 1], 0.0, term)
        last_out[g] = jnp.where(half == 0, totals[1], totals[0]).astype(bf16)
        partial[g, 0, 0] = jnp.where(half == 0, totals[0], totals[1])
        dswap(g).start()

    def finish(g):
        dswap(g).wait_recv()
        here, there = partial[g, 0, 0], last_in[g].astype(f32)
        dkv[g, 0] = (partial[g, 1, 0] + jnp.where(half == 0, here, there)).astype(bf16)
        dkv[g, 1] = (partial[g, 1, 1] + jnp.where(half == 0, there, here)).astype(bf16)

    chain = (gradients, collect, send_back, add_up, finish)

    def step(s, _):
        for lag, stage in enumerate(chain):
            @pl.when((s >= lag) & (s < kv_heads + lag))
            def _():
                stage(s - lag)
        return 0
    lax.fori_loop(0, kv_heads + len(chain) - 1, step, 0)

    def drain(g):
        for c in (swap(g), prev(g), dprev(g), dswap(g)):
            c.wait_send()
        for d in range(1, copies):
            pick(g, d).wait_send()
            dpick(g, d).wait_send()
        for t in range(1, blocks):
            ring(g, t, True).wait_send()
            dring(g, t).wait_send()
    each(drain)


def shards(copies, blocks, queries, keys, values, attention_out, out_grad, span_order, doc_lengths):
    rows, heads, width = queries.shape
    kv_heads = keys.shape[1]
    group = heads // kv_heads
    lanes, keys_seen = rows * group, (blocks + 1) * rows
    split = (rows, kv_heads, group, width)
    kv = jnp.stack([jnp.transpose(keys, (1, 0, 2)), jnp.transpose(values, (1, 0, 2))], axis=1)
    bf16, f32 = jnp.bfloat16, jnp.float32
    block, pair = (rows, width), (2, rows, width)
    dma = pltpu.SemaphoreType.DMA
    one, over_q, over_j = (kv_heads,), (kv_heads, copies - 1), (kv_heads, blocks - 1)
    vmem, smem = pl.BlockSpec(memory_space=pltpu.VMEM), pl.BlockSpec(memory_space=pltpu.SMEM)
    work = kv_heads * lanes * keys_seen
    dquery, dkv = pl.pallas_call(
        functools.partial(kernel, (copies, blocks)),
        out_shape=(jax.ShapeDtypeStruct(split, bf16), jax.ShapeDtypeStruct(kv.shape, bf16)),
        in_specs=[smem, smem, vmem, vmem, vmem, vmem],
        out_specs=(vmem, vmem),
        scratch_shapes=[
            pltpu.VMEM((kv_heads, blocks + 1) + pair, bf16),
            pltpu.VMEM((kv_heads, copies + 1) + block, bf16),
            pltpu.VMEM(over_q + block, bf16),
            pltpu.VMEM(one + block, bf16),
            pltpu.VMEM((keys_seen, lanes), f32),
            pltpu.VMEM((kv_heads, 1, lanes), f32),
            pltpu.VMEM((lanes, width), bf16),
            pltpu.VMEM((lanes, width), bf16),
            pltpu.VMEM((keys_seen, lanes), bf16),
            pltpu.VMEM((keys_seen, lanes), bf16),
            pltpu.VMEM((kv_heads, 2) + pair, f32),
            pltpu.VMEM(over_j + pair, bf16),
            pltpu.VMEM(over_j + pair, bf16),
            pltpu.VMEM(one + block, bf16),
            pltpu.VMEM(one + block, bf16),
            pltpu.VMEM(one + block, bf16),
            pltpu.VMEM(over_q + block, bf16),
            pltpu.VMEM(over_q + block, bf16),
            pltpu.VMEM(one + block, bf16),
            pltpu.VMEM(one + block, bf16),
            dma(one), dma(one), dma(over_q), dma(over_q), dma(one), dma(one), dma(over_j), dma(over_j),
            dma(over_j), dma(over_j), dma(one), dma(one), dma(over_q), dma(over_q), dma(one), dma(one),
        ],
        compiler_params=pltpu.CompilerParams(
            collective_id=0, has_side_effects=True, vmem_limit_bytes=48 * 1024 * 1024),
        cost_estimate=pl.CostEstimate(
            flops=10 * work * width, bytes_accessed=8 * rows * heads * width, transcendentals=work),
        name="attention_grads",
    )(span_order, doc_lengths, kv, queries.reshape(split), attention_out.reshape(split), out_grad.reshape(split))
    grads = jnp.transpose(dkv, (1, 2, 0, 3))
    return dquery.reshape(queries.shape), grads[0], grads[1]


def solution(mesh):
    spread = P(("query", "head"), None, None)
    return jax.shard_map(
        functools.partial(shards, mesh.shape["query"], mesh.shape["head"] // 2),
        mesh=mesh,
        in_specs=(spread,) * 5 + (P(), P()),
        out_specs=(spread,) * 3,
        check_vma=False,
    )
```

```python
import functools
import math

import jax
import jax.numpy as jnp
from jax import lax
from jax.experimental import pallas as pl
from jax.experimental.pallas import tpu as pltpu
from jax.sharding import PartitionSpec as P

masked = -1e30


def kernel(sizes, order, lengths, kv, query_far, out_far, grad_far, dquery, dkv, query, out_fwd, grad, window, cand,
           cross_out, cross_in, bias, delta, q_rows, g_rows, p_tile, s_tile, partial, sent, came, half_out, half_in,
           back_out, back_in, load_s, pick_s, pick_r, cross_s, cross_r, ring_s, ring_r,
           dring_s, dring_r, dcross_s, dcross_r, dpick_s, dpick_r):
    copies, blocks = sizes
    kv_heads, _, rows, width = kv.shape
    group = query.shape[2]
    lanes = rows * group
    keys_seen = (blocks + 1) * rows
    chunk = min(256, lanes)
    token_chunk = chunk // group
    factor = width ** -0.5
    f32, bf16 = jnp.float32, jnp.bfloat16

    mine = lax.axis_index("query")
    head = lax.axis_index("head")
    half, place = lax.div(head, blocks), lax.rem(head, blocks)
    other = 1 - half
    sibling = {"head": other * blocks + place}

    def ahead(d):
        return lax.rem(mine + d, copies)

    def behind(d):
        return lax.rem(mine + (copies - d), copies)

    def lower(t):
        return {"head": half * blocks + lax.rem(place + (blocks - t), blocks)}

    def upper(t):
        return {"head": half * blocks + lax.rem(place + t, blocks)}

    def copy(src, dst, send, recv, to):
        return pltpu.make_async_remote_copy(
            src_ref=src, dst_ref=dst, send_sem=send, recv_sem=recv, device_id=to,
            device_id_type=pl.DeviceIdType.MESH)

    loads = [pltpu.make_async_copy(far, near, load_s.at[i]) for i, (far, near) in
             enumerate(((query_far, query), (out_far, out_fwd), (grad_far, grad)))]
    for load in loads:
        load.start()

    barrier = pltpu.get_barrier_semaphore()
    partners = [sibling]
    partners += [{"query": ahead(d)} for d in range(1, copies)]
    partners += [upper(t) for t in range(1, blocks)]
    for to in partners:
        pl.semaphore_signal(barrier, inc=1, device_id=to, device_id_type=pl.DeviceIdType.MESH)
    pl.semaphore_wait(barrier, len(partners))

    def pick(g, d):
        return copy(kv.at[g], cand.at[g, d - 1], pick_s.at[g, d - 1], pick_r.at[g, d - 1], {"query": ahead(d)})

    def cross(g):
        return copy(cross_out.at[g], cross_in.at[g], cross_s.at[g], cross_r.at[g], sibling)

    def ring(g, t, own):
        src = kv.at[g] if own else window.at[g, 0]
        return copy(src, window.at[g, t], ring_s.at[g, t - 1], ring_r.at[g, t - 1], lower(t))

    def dring(g, t):
        return copy(sent.at[g, t - 1], came.at[g, t - 1], dring_s.at[g, t - 1], dring_r.at[g, t - 1], upper(t))

    def dcross(g):
        return copy(half_out.at[g], half_in.at[g], dcross_s.at[g], dcross_r.at[g], sibling)

    def dpick(g, d):
        return copy(back_out.at[g, d - 1], back_in.at[g, d - 1], dpick_s.at[g, d - 1], dpick_r.at[g, d - 1],
                    {"query": behind(d)})

    def each(body):
        def step(g, _):
            body(g)
            return 0
        lax.fori_loop(0, kv_heads, step, 0)

    def source(which):
        wanted = order[mine, which] - 1
        distance, side = jnp.int32(-1), jnp.int32(0)
        for d in range(copies):
            there = behind(d)
            for i in range(2):
                hit = order[there, i] == wanted
                distance, side = jnp.where(hit, d, distance), jnp.where(hit, i, side)
        return distance, side

    far_here, side_here = source(half)
    far_other, side_other = source(other)

    def outgoing(g):
        for d in range(1, copies):
            pick(g, d).start()
    each(outgoing)

    def first(g):
        for t in range(1, blocks):
            @pl.when(place < t)
            def _():
                ring(g, t, True).start()
    each(first)

    begin = order[mine, half] * (blocks * rows) + place * rows
    row = lax.div(lax.broadcasted_iota(jnp.int32, (1, lanes), 1), jnp.int32(group))
    pos = begin + row

    def bound(i, carry):
        end, low = carry
        end = end + lengths[i]
        return end, jnp.where(pos >= end, end, low)

    _, low = lax.fori_loop(0, lengths.shape[0] - 1, bound, (jnp.int32(0), jnp.zeros_like(pos)))
    low = low - begin + blocks * rows

    for c in range(0, lanes, chunk):
        at = lax.broadcasted_iota(jnp.int32, (keys_seen, chunk), 0)
        seen = (at >= low[:, c:c + chunk]) & (at <= row[:, c:c + chunk] + blocks * rows)
        bias[:, c:c + chunk] = jnp.where(seen, 0.0, masked)

    for load in loads:
        load.wait()

    def own_and_delta(g):
        window[g, blocks] = kv[g]
        product = out_fwd[:, g].astype(f32) * grad[:, g].astype(f32)
        delta[g] = jnp.sum(product.reshape(lanes, width).T, axis=0, keepdims=True)

    def exchange(g):
        for d in range(1, copies):
            pick(g, d).wait_recv()
        here = there = kv[g].astype(f32)
        for d in range(1, copies):
            block = cand[g, d - 1].astype(f32)
            here, there = jnp.where(far_here == d, block, here), jnp.where(far_other == d, block, there)
        cross_out[g] = there.astype(bf16)
        cross(g).start()
        window[g, 0] = here.astype(bf16)
        own_and_delta(g)

    def spread(g):
        cross(g).wait_recv()
        window[g, 0] = jnp.where(side_here == half, window[g, 0].astype(f32), cross_in[g].astype(f32)).astype(bf16)
        for t in range(1, blocks):
            @pl.when(place >= t)
            def _():
                ring(g, t, False).start()

    def gradients(g):
        for t in range(1, blocks):
            ring(g, t, True).wait_recv()
        q_rows[...] = query[:, g].astype(f32).reshape(lanes, width).astype(bf16)
        g_rows[...] = grad[:, g].astype(f32).reshape(lanes, width).astype(bf16)
        key = window[g, :, 0].reshape(keys_seen, width)
        value = window[g, :, 1].reshape(keys_seen, width)
        key_t = key.astype(f32).T.astype(bf16)
        across = (((1,), (1,)), ((), ()))
        for c in range(0, lanes, chunk):
            cols = slice(c, c + chunk)
            score = lax.dot_general(key, q_rows[cols, :], across, preferred_element_type=f32)
            score = score * (factor * math.log2(math.e)) + bias[:, cols]
            power = jnp.exp2(score - jnp.max(score, axis=0, keepdims=True))
            prob = power * (1.0 / jnp.sum(power, axis=0, keepdims=True))
            grad_prob = lax.dot_general(value, g_rows[cols, :], across, preferred_element_type=f32)
            grad_score = (prob * (grad_prob - delta[g, :, cols])).astype(bf16)
            p_tile[:, cols] = prob.astype(bf16)
            s_tile[:, cols] = grad_score
            dq = jnp.dot(key_t, grad_score, preferred_element_type=f32).T * factor
            first_token = c // group
            dquery[first_token:first_token + token_chunk, g] = dq.reshape(token_chunk, group, width).astype(bf16)
        dk = jnp.dot(s_tile[...], q_rows[...], preferred_element_type=f32) * factor
        dv = jnp.dot(p_tile[...], g_rows[...], preferred_element_type=f32)
        for kind, total in enumerate((dk, dv)):
            total = total.reshape(blocks + 1, rows, width)
            partial[g, 0, kind] = total[0]
            partial[g, 1, kind] = total[blocks]
            sent[g, :, kind] = total[1:blocks].astype(bf16)
        for t in range(1, blocks):
            dring(g, t).start()

    def collect(g):
        earlier, own = partial[g, 0], partial[g, 1]
        for t in range(1, blocks):
            dring(g, t).wait_recv()
            term = came[g, t - 1].astype(f32)
            earlier = earlier + jnp.where(place >= t, term, 0.0)
            own = own + jnp.where(place < t, term, 0.0)
        partial[g, 0], partial[g, 1] = earlier, own
        half_out[g] = earlier.astype(bf16)
        dcross(g).start()

    def send_back(g):
        dcross(g).wait_recv()
        here, there = partial[g, 0], half_in[g].astype(f32)

        def owed(d):
            return (jnp.where((far_here == d) & (side_here == half), here, 0.0)
                    + jnp.where((far_other == d) & (side_other == half), there, 0.0))

        for d in range(1, copies):
            back_out[g, d - 1] = owed(d).astype(bf16)
            dpick(g, d).start()
        partial[g, 1] = partial[g, 1] + owed(0)

    def finish(g):
        total = partial[g, 1]
        for d in range(1, copies):
            dpick(g, d).wait_recv()
            total = total + back_in[g, d - 1].astype(f32)
        dkv[g] = total.astype(bf16)

    chain = ((0, exchange), (1, spread), (2, gradients), (3, collect), (4, send_back), (5, finish))

    def step(s, _):
        for lag, stage in chain:
            @pl.when((s >= lag) & (s < kv_heads + lag))
            def _():
                stage(s - lag)
        return 0
    lax.fori_loop(0, kv_heads + chain[-1][0], step, 0)

    def drain(g):
        for c in (cross(g), dcross(g)):
            c.wait_send()
        for d in range(1, copies):
            pick(g, d).wait_send()
            dpick(g, d).wait_send()
        for t in range(1, blocks):
            ring(g, t, True).wait_send()
            dring(g, t).wait_send()
    each(drain)


def shards(copies, blocks, queries, keys, values, attention_out, out_grad, span_order, doc_lengths):
    rows, heads, width = queries.shape
    kv_heads = keys.shape[1]
    group = heads // kv_heads
    lanes, keys_seen = rows * group, (blocks + 1) * rows
    split = (rows, kv_heads, group, width)
    kv = jnp.stack([jnp.transpose(keys, (1, 0, 2)), jnp.transpose(values, (1, 0, 2))], axis=1)
    bf16, f32 = jnp.bfloat16, jnp.float32
    pair = (2, rows, width)
    dma = pltpu.SemaphoreType.DMA
    one, over_q, over_j = (kv_heads,), (kv_heads, copies - 1), (kv_heads, blocks - 1)
    vmem, smem = pl.BlockSpec(memory_space=pltpu.VMEM), pl.BlockSpec(memory_space=pltpu.SMEM)
    far = pl.BlockSpec(memory_space=pl.ANY)
    work = kv_heads * lanes * keys_seen
    dquery, dkv = pl.pallas_call(
        functools.partial(kernel, (copies, blocks)),
        out_shape=(jax.ShapeDtypeStruct(split, bf16), jax.ShapeDtypeStruct(kv.shape, bf16)),
        in_specs=[smem, smem, vmem, far, far, far],
        out_specs=(vmem, vmem),
        scratch_shapes=[
            pltpu.VMEM(split, bf16),
            pltpu.VMEM(split, bf16),
            pltpu.VMEM(split, bf16),
            pltpu.VMEM((kv_heads, blocks + 1) + pair, bf16),
            pltpu.VMEM(over_q + pair, bf16),
            pltpu.VMEM(one + pair, bf16),
            pltpu.VMEM(one + pair, bf16),
            pltpu.VMEM((keys_seen, lanes), f32),
            pltpu.VMEM((kv_heads, 1, lanes), f32),
            pltpu.VMEM((lanes, width), bf16),
            pltpu.VMEM((lanes, width), bf16),
            pltpu.VMEM((keys_seen, lanes), bf16),
            pltpu.VMEM((keys_seen, lanes), bf16),
            pltpu.VMEM((kv_heads, 2) + pair, f32),
            pltpu.VMEM(over_j + pair, bf16),
            pltpu.VMEM(over_j + pair, bf16),
            pltpu.VMEM(one + pair, bf16),
            pltpu.VMEM(one + pair, bf16),
            pltpu.VMEM(over_q + pair, bf16),
            pltpu.VMEM(over_q + pair, bf16),
            dma((3,)), dma(over_q), dma(over_q), dma(one), dma(one), dma(over_j), dma(over_j),
            dma(over_j), dma(over_j), dma(one), dma(one), dma(over_q), dma(over_q),
        ],
        compiler_params=pltpu.CompilerParams(
            collective_id=0, has_side_effects=True, vmem_limit_bytes=48 * 1024 * 1024),
        cost_estimate=pl.CostEstimate(
            flops=10 * work * width, bytes_accessed=8 * rows * heads * width, transcendentals=work),
        name="attention_grads",
    )(span_order, doc_lengths, kv, queries.reshape(split), attention_out.reshape(split), out_grad.reshape(split))
    grads = jnp.transpose(dkv, (1, 2, 0, 3))
    return dquery.reshape(queries.shape), grads[0], grads[1]


def solution(mesh):
    spread = P(("query", "head"), None, None)
    return jax.shard_map(
        functools.partial(shards, mesh.shape["query"], mesh.shape["head"] // 2),
        mesh=mesh,
        in_specs=(spread,) * 5 + (P(), P()),
        out_specs=(spread,) * 3,
        check_vma=False,
    )
```
